32 devices in a mesh: groups: 2 (over y), shot: 8 (over z, x), ap: 2 (over core).
Axes of the slice: x: 2, y: 2, z: 4, core: 2. Of those that a mesh axis runs over, the one named last changes fastest.
Arguments:
- forward_field: bfloat16 [16, 16, 64, 128], P(('groups', 'shot'), 'ap'), parts along dimension 0, may hold values from -6 to 6
- forward_older: bfloat16 [16, 16, 64, 128], P(('groups', 'shot'), 'ap'), parts along dimension 0, may hold values from -6 to 6
- adjoint_field: bfloat16 [16, 16, 64, 128], P(('groups', 'shot'), 'ap'), parts along dimension 0, may hold values from -6 to 6
- adjoint_newer: bfloat16 [16, 16, 64, 128], P(('groups', 'shot'), 'ap'), parts along dimension 0, may hold values from -6 to 6
- velocity: float32 [32, 128, 192], P(('groups', 'ap'), 'shot'), parts along dimension 0, may hold values from 0.15 to 0.4
- anchor_first: int32 [16], P(('groups', 'shot')), parts along dimension 0, may hold values from 0 to 64
- anchor_second: int32 [16], P(('groups', 'shot')), parts along dimension 0, may hold values from 0 to 64
- wavelet: float32 [16, 4], P(('groups', 'shot')), parts along dimension 0, may hold values from -48 to 48
- source_cell: int32 [16], P(('groups', 'shot')), parts along dimension 0, may hold values from 0 to 131071
- receivers: int32 [16, 256], P(('groups', 'shot')), parts along dimension 0, may hold values from 0 to 131071
- traces: float32 [16, 4, 256], P(('groups', 'shot')), parts along dimension 0, may hold values from -24 to 24
Outputs:
- migrated_image: float32 [32, 128, 192], P(('groups', 'ap'), 'shot'), parts along dimension 0
The draws below stay inside these ranges and needn't reach their ends.
There are 2 independent parts, one for each index of `groups`. The reference program is written for one: setup_inputs(seed, part) draws one part's arguments, and reference() takes and returns one part's arrays. A program takes and returns all parts, laid end to end along the dimension named above; each array names one. Nothing has to cross between parts.
All inputs are finite; a program needn't handle non-finite values.
Results may differ from the reference program's by a relative error of at most 0.0003.
Values may be sent and summed in bfloat16 or wider, within the bound.
A program may use at most 64 MiB of HBM per device.

```python
import jax
import jax.numpy as jnp
from jax import lax

AZ = 16
AX = 64
AY = 128
STEPS = 4
NREC = 256
SHOTS = 8
GX = 128
GY = 192


def with_ends(array, key, low, largest):
    longest = array.shape.index(max(array.shape))
    spots = []
    for shift in (0, 1):
        where = [jax.random.randint(jax.random.fold_in(key, axis), (), 0, length) for axis, length in enumerate(array.shape)]
        where[longest] = (where[longest] + shift) % array.shape[longest]
        spots.append(tuple(where))
    return array.at[spots[0]].set(low).at[spots[1]].set(largest)


def steps_of(rng, extent, pieces, smallest, largest):
    level, own = 1.0, jax.random.fold_in(rng, 6)
    for position, shards_of in pieces:
        steps = jnp.exp(jax.random.uniform(jax.random.fold_in(own, position), (shards_of,), jnp.float32, smallest / len(pieces), largest / len(pieces)))
        level = level * jnp.repeat(steps, extent[position] // shards_of).reshape([-1 if axis == position else 1 for axis in range(len(extent))])
    return level


def bell_draw(own_key, dims, scale, bound, shards=(), dtype=jnp.bfloat16):
    entries = jax.random.normal(own_key, dims, jnp.float32) * scale
    if len(shards) > 0:
        entries = steps_of(own_key, dims, shards, -0.22, 0.18) * entries
    return jnp.clip(entries, min=-bound, max=bound).astype(dtype)


def setup_inputs(seed: int = 0, part: int = 0) -> dict:
    arg_keys = jax.random.split(jax.random.key(seed), 12)
    part_splits = jax.random.split(jax.random.fold_in(arg_keys[11], part), 12)
    return {
        "forward_field": bell_draw(part_splits[0], (SHOTS, AZ, AX, AY), 1.0, 6.0, ((0, 8), (1, 2))),
        "forward_older": bell_draw(part_splits[1], (SHOTS, AZ, AX, AY), 1.0, 6.0, ((0, 8), (1, 2))),
        "adjoint_field": bell_draw(part_splits[2], (SHOTS, AZ, AX, AY), 1.0, 6.0, ((0, 8), (1, 2))),
        "adjoint_newer": bell_draw(part_splits[3], (SHOTS, AZ, AX, AY), 1.0, 6.0, ((0, 8), (1, 2))),
        "velocity": jnp.clip(0.15 + 0.25 * jax.random.uniform(part_splits[4], (AZ, GX, GY), jnp.float32) ** steps_of(part_splits[4], (AZ, GX, GY), ((0, 2), (1, 8)), -0.2, 0.2), 0.15, 0.4),
        "anchor_first": with_ends(jax.random.randint(part_splits[5], (SHOTS,), 0, GX - AX + 1), jax.random.fold_in(part_splits[5], 1), 0, GX - AX).astype(jnp.int32),
        "anchor_second": with_ends(jax.random.randint(part_splits[6], (SHOTS,), 0, GY - AY + 1), jax.random.fold_in(part_splits[6], 1), 0, GY - AY).astype(jnp.int32),
        "wavelet": bell_draw(part_splits[7], (SHOTS, STEPS), 8.0, 48.0, ((0, 8),), jnp.float32),
        "source_cell": with_ends(jax.random.randint(part_splits[8], (SHOTS,), 0, AZ * AX * AY), jax.random.fold_in(part_splits[8], 1), 0, (AZ * AX * AY) - 1).astype(jnp.int32),
        "receivers": with_ends(jax.random.randint(part_splits[9], (SHOTS, NREC), 0, AZ * AX * AY), jax.random.fold_in(part_splits[9], 1), 0, (AZ * AX * AY) - 1).astype(jnp.int32),
        "traces": bell_draw(part_splits[10], (SHOTS, STEPS, NREC), 4.0, 24.0, ((0, 8),), jnp.float32),
    }


STENCIL = (-205.0 / 72.0, 8.0 / 5.0, -1.0 / 5.0, 8.0 / 315.0, -1.0 / 560.0)


def laplace(field):
    depth, first, second = field.shape
    padded = jnp.pad(field, 4)

    def shifted(dz, dx, dy):
        return padded[4 + dz:4 + dz + depth, 4 + dx:4 + dx + first, 4 + dy:4 + dy + second]

    summed = (3.0 * STENCIL[0]) * field
    for reach in range(1, 5):
        summed = summed + STENCIL[reach] * (shifted(reach, 0, 0) + shifted(-reach, 0, 0) + shifted(0, reach, 0) + shifted(0, -reach, 0) + shifted(0, 0, reach) + shifted(0, 0, -reach))
    return summed


def excite(cells, amounts):
    flat = jnp.zeros((AZ * AX * AY,), jnp.float32).at[cells].add(amounts)
    return flat.reshape(AZ, AX, AY)


def reference(forward_field, forward_older, adjoint_field, adjoint_newer, velocity, anchor_first, anchor_second, wavelet, source_cell, receivers, traces):
    def one_shot(image_sum, inputs):
        f_now, f_old, a_now, a_new, first, second, pulse, source, cells, records = inputs
        window = lax.dynamic_slice(velocity, (first * 0, first, second), (AZ, AX, AY))
        coefficient = window * window
        current = f_now.astype(jnp.float32)
        previous = f_old.astype(jnp.float32)
        forward_states = []
        for t in range(STEPS):
            updated = 2.0 * current - previous + coefficient * (laplace(current) + excite(source[None], pulse[t][None]))
            previous, current = current, updated
            forward_states.append(current)
        current = a_now.astype(jnp.float32)
        following = a_new.astype(jnp.float32)
        adjoint_states = [None] * STEPS
        for t in range(STEPS, 0, -1):
            updated = 2.0 * current - following + coefficient * (laplace(current) + excite(cells, records[t - 1]))
            following, current = current, updated
            adjoint_states[t - 1] = current
        correlation = forward_states[0] * adjoint_states[0]
        for t in range(1, STEPS):
            correlation = correlation + forward_states[t] * adjoint_states[t]
        shot_image = correlation / STEPS
        start = (first * 0, first, second)
        region = lax.dynamic_slice(image_sum, start, (AZ, AX, AY))
        return lax.dynamic_update_slice(image_sum, region + shot_image, start), None

    initial = jnp.zeros((AZ, GX, GY), jnp.float32)
    result, unused = lax.scan(one_shot, initial, (forward_field, forward_older, adjoint_field, adjoint_newer, anchor_first, anchor_second, wavelet, source_cell, receivers, traces))
    return result
```

```python
import jax
import jax.numpy as jnp
from jax import lax
from jax.experimental import pallas as pl
from jax.experimental.pallas import tpu as pltpu
from jax.sharding import PartitionSpec as P

STEPS = 4
GX = 128
GY = 192


STENCIL = (-205.0 / 72.0, 8.0 / 5.0, -1.0 / 5.0, 8.0 / 315.0, -1.0 / 560.0)


def with_halo(shard, sides, width):
    for axis, dim in sides:
        count, length = (lax.axis_size(axis), shard.shape[dim])
        up = [(i, (i + 1) % count) for i in range(count - 1)]
        down = [(j, i) for i, j in up]
        last = lax.slice_in_dim(shard, length - width, length, axis=dim)
        initial = lax.slice_in_dim(shard, 0, width, axis=dim)
        before = lax.ppermute(last, axis, up)
        after = lax.ppermute(initial, axis, down)
        shard = jnp.concatenate([before, shard, after], axis=dim)
    return shard


def laplace_rows(extended):
    row_count = extended.shape[1] - 8
    width_x = extended.shape[2]
    width_y = extended.shape[3]
    padded = jnp.pad(extended, ((0, 0), (0, 0), (4, 4), (4, 4)))

    def shifted(dz, dx, dy):
        return padded[
            :, 4 + dz : 4 + dz + row_count, 4 + dx : 4 + dx + width_x, 4 + dy : 4 + dy + width_y
        ]

    summed = 3.0 * STENCIL[0] * shifted(0, 0, 0)
    for reach in range(1, 5):
        summed = summed + STENCIL[reach] * (
            shifted(reach, 0, 0)
            + shifted(-reach, 0, 0)
            + shifted(0, reach, 0)
            + shifted(0, -reach, 0)
            + shifted(0, 0, reach)
            + shifted(0, 0, -reach)
        )
    return summed


def inject(cells, amounts, start_row, row_count, width_x, width_y):
    plane = width_x * width_y
    offset_cells = cells - start_row * plane
    inside = (offset_cells >= 0) & (offset_cells < row_count * plane)
    flat = (
        jnp.zeros((row_count * plane,), jnp.float32)
        .at[jnp.where(inside, offset_cells, 0)]
        .add(jnp.where(inside, amounts, 0.0))
    )
    return flat.reshape(row_count, width_x, width_y)


def sources_for(injections, start_row, row_count, width_x, width_y):
    return jnp.stack(
        [
            inject(cells, amounts, start_row, row_count, width_x, width_y)
            for cells, amounts in injections
        ]
    )


def advance(current, previous, coefficient, injections, first_row):
    slab_rows, width_x, width_y = (current.shape[1], current.shape[2], current.shape[3])
    extended = with_halo(current, (("ap", 1),), 4)
    sources = sources_for(injections, first_row, slab_rows, width_x, width_y)
    return 2.0 * current - previous + coefficient[None] * (laplace_rows(extended) + sources)


def march(current, previous, coefficient, injections_at, first_row):
    snapshots = []
    for t in range(STEPS):
        updated = advance(current, previous, coefficient, injections_at(t), first_row)
        previous, current = (current, updated)
        snapshots.append(current)
    return snapshots


def shards(
    forward_field,
    forward_older,
    adjoint_field,
    adjoint_newer,
    velocity,
    anchor_first,
    anchor_second,
    wavelet,
    source_cell,
    receivers,
    traces,
):
    slab_rows, width_x, width_y = (
        forward_field.shape[1],
        forward_field.shape[2],
        forward_field.shape[3],
    )
    first_row = lax.axis_index("ap") * slab_rows
    anchor = anchor_first[0] * 0
    speed_model = lax.all_gather(velocity, "shot", axis=1, tiled=True)
    window = lax.dynamic_slice(
        speed_model, (anchor, anchor_first[0], anchor_second[0]), (slab_rows, width_x, width_y)
    )
    coefficient = window * window
    f_now, f_old, a_now, a_new = (forward_field, forward_older, adjoint_field, adjoint_newer)

    def forward_source(t):
        return (source_cell, wavelet[0, t : t + 1])

    def adjoint_source(t):
        return (receivers[0], traces[0, STEPS - 1 - t])

    forward_snaps = march(
        f_now.astype(jnp.float32),
        f_old.astype(jnp.float32),
        coefficient,
        lambda t: [forward_source(t)],
        first_row,
    )
    adjoint_snaps = march(
        a_now.astype(jnp.float32),
        a_new.astype(jnp.float32),
        coefficient,
        lambda t: [adjoint_source(t)],
        first_row,
    )
    forward_states = [state[0] for state in forward_snaps]
    adjoint_states = [state[0] for state in adjoint_snaps]
    correlation = forward_states[0] * adjoint_states[STEPS - 1]
    for t in range(1, STEPS):
        correlation = correlation + forward_states[t] * adjoint_states[STEPS - 1 - t]
    shot_image = correlation / STEPS
    partial_image = lax.dynamic_update_slice(
        jnp.zeros((slab_rows, GX, GY), jnp.float32),
        shot_image,
        (anchor, anchor_first[0], anchor_second[0]),
    )
    return lax.psum_scatter(partial_image, "shot", scatter_dimension=1, tiled=True)


SLAB, AX, AY = 8, 64, 128
COLUMNS, LEVELS = 2, 4
SHOTS = COLUMNS * LEVELS
ROWS = GX // SHOTS
TAIL = GY - AY
PAD = 8
REACH = 4
MESH = pl.DeviceIdType.MESH


def window_kernel(
    a_ref,
    b_ref,
    wavelet_ref,
    source_ref,
    receivers_ref,
    traces_ref,
    forward_ref,
    forward_older_ref,
    adjoint_ref,
    adjoint_newer_ref,
    velocity_ref,
    out_ref,
    state,
    model,
    coefficient,
    injected,
    placed,
    outgoing,
    incoming,
    offsets,
    offset_tile,
    halo_send,
    halo_recv,
    model_send,
    model_recv,
    image_send,
    image_recv,
    offset_send,
    offset_recv,
):
    half = lax.axis_index("ap")
    me = lax.axis_index("shot")
    level, column = me // COLUMNS, me % COLUMNS

    barrier = pltpu.get_barrier_semaphore()
    pl.semaphore_signal(barrier, inc=1, device_id={"ap": 1 - half}, device_id_type=MESH)
    for away in range(1, SHOTS):
        pl.semaphore_signal(
            barrier, inc=1, device_id={"shot": (me + away) % SHOTS}, device_id_type=MESH
        )

    a = a_ref[0]
    b = b_ref[0]
    lane = lax.broadcasted_iota(jnp.int32, (1, AY), 1)

    mine = pl.ds(pl.multiple_of(me * ROWS, ROWS), ROWS)
    for z in range(SLAB):
        model[z, mine, :] = velocity_ref[z, :, 0:AY]
    for z in range(SLAB // 2):
        model[SLAB + z, mine, :] = jnp.concatenate(
            [velocity_ref[z, :, AY:GY], velocity_ref[z + SLAB // 2, :, AY:GY]], axis=1
        )
    offset_tile[...] = jnp.full((8, AY), b, jnp.int32)

    pl.semaphore_wait(barrier, SHOTS)

    def model_copy(block, slot, target):
        rows = pl.ds(pl.multiple_of(block * ROWS, ROWS), ROWS)
        return pltpu.make_async_remote_copy(
            src_ref=model.at[:, rows, :],
            dst_ref=model.at[:, rows, :],
            send_sem=model_send.at[slot],
            recv_sem=model_recv.at[block],
            device_id={"shot": target},
            device_id_type=MESH,
        )

    across = level * COLUMNS + 1 - column
    model_copies = []
    for away in range(1, LEVELS):
        copy = model_copy(me, away, (level + away) % LEVELS * COLUMNS + column)
        copy.start()
        model_copies.append(copy)
    copy = model_copy(me, 0, across)
    copy.start()
    model_copies.append(copy)

    offset_copies = []
    for away in range(1, SHOTS):
        copy = pltpu.make_async_remote_copy(
            src_ref=offset_tile,
            dst_ref=offsets.at[me],
            send_sem=offset_send.at[away],
            recv_sem=offset_recv.at[away],
            device_id={"shot": (me + away) % SHOTS},
            device_id_type=MESH,
        )
        copy.start()
        offset_copies.append(copy)
    offsets[me] = offset_tile[...]

    outer = pl.ds((REACH + SLAB) * (half), REACH)
    inner = pl.ds(PAD, AX)
    for f, (older, now) in enumerate(
        ((forward_older_ref, forward_ref), (adjoint_newer_ref, adjoint_ref))
    ):
        for k in range(1, STEPS + 1):

            def clear(z, carry):
                state[f, k, z + REACH, 0:PAD, :] = jnp.zeros((PAD, AY), jnp.float32)
                state[f, k, z + REACH, PAD + AX :, :] = jnp.zeros((PAD, AY), jnp.float32)
                return carry

            lax.fori_loop(0, SLAB, clear, 0)
            state[f, k, outer, inner, :] = jnp.zeros((REACH, AX, AY), jnp.float32)

        def load(z, carry):
            state[f, 0, z + REACH, inner, :] = older[0, z].astype(jnp.float32)
            state[f, 1, z + REACH, inner, :] = now[0, z].astype(jnp.float32)
            return carry

        lax.fori_loop(0, SLAB, load, 0)

    def halo_copy(f, k):
        return pltpu.make_async_remote_copy(
            src_ref=state.at[f, k, pl.ds(2 * REACH - REACH * half, REACH), inner, :],
            dst_ref=state.at[f, k, pl.ds((REACH + SLAB) * half, REACH), inner, :],
            send_sem=halo_send.at[f, k - 1],
            recv_sem=halo_recv.at[f, k - 1],
            device_id={"ap": 1 - half},
            device_id_type=MESH,
        )

    halos = {}
    for f in range(2):
        halos[f, 1] = halo_copy(f, 1)
        halos[f, 1].start()

    cells = receivers_ref[...]
    count = cells.shape[1]
    row_of = cells // AY - half * (SLAB * AX)
    lane_of = cells % AY
    hot_rows = jnp.where(
        lax.broadcasted_iota(jnp.int32, (SLAB * AX, count), 0) == row_of, 1.0, 0.0
    ).astype(jnp.bfloat16)
    hot_lanes = lax.broadcasted_iota(jnp.int32, (AY, count), 0) == lane_of
    for k in range(STEPS):
        amounts = jnp.where(hot_lanes, traces_ref[0, STEPS - 1 - k : STEPS - k, :], 0.0)
        upper = amounts.astype(jnp.bfloat16)
        lower = (amounts - upper.astype(jnp.float32)).astype(jnp.bfloat16)
        both = lax.dot_general(
            hot_rows,
            jnp.concatenate([upper, lower], axis=0),
            (((1,), (1,)), ((), ())),
            preferred_element_type=jnp.float32,
        )
        injected[k] = (both[:, :AY] + both[:, AY:]).reshape(SLAB, AX, AY)

    def blank(z, carry):
        placed[z, 0:AX, :] = jnp.zeros((AX, AY), jnp.float32)
        placed[z, 2 * AX :, :] = jnp.zeros((GX - AX, AY), jnp.float32)
        return carry

    lax.fori_loop(0, SLAB, blank, 0)

    for away in range(1, LEVELS):
        block = (level + LEVELS - away) % LEVELS * COLUMNS + column
        model_copy(block, 0, across).wait_recv()
        copy = model_copy(block, LEVELS - 1 + away, across)
        copy.start()
        model_copies.append(copy)
    for away in range(LEVELS):
        block = (level + LEVELS - away) % LEVELS * COLUMNS + 1 - column
        model_copy(block, 0, across).wait_recv()

    def square(z, carry):
        rows = pl.ds(a, AX)
        for part in range(2):
            tail = model[SLAB + z, rows, :]
            if part:
                tail = pltpu.roll(tail, TAIL, 1)
            joined = jnp.where(lane >= b, model[z + part * (SLAB // 2), rows, :], tail)
            window = pltpu.roll(joined, (AY - b) % AY, 1)
            coefficient[z + part * (SLAB // 2)] = window * window
        return carry

    lax.fori_loop(0, SLAB // 2, square, 0)

    flat = (
        lax.broadcasted_iota(jnp.int32, (AX, AY), 0) * AY
        + lax.broadcasted_iota(jnp.int32, (AX, AY), 1)
    )

    def layers(f, k, first):
        def layer(i, carry):
            z = first + i
            slot = z + REACH
            centre = state[f, k + 1, slot, inner, :]
            total = (3.0 * STENCIL[0]) * centre
            for reach in range(1, REACH + 1):
                near = state[f, k + 1, slot + reach, inner, :]
                near = near + state[f, k + 1, slot - reach, inner, :]
                near = near + state[f, k + 1, slot, pl.ds(PAD + reach, AX), :]
                near = near + state[f, k + 1, slot, pl.ds(PAD - reach, AX), :]
                near = near + jnp.where(lane >= reach, pltpu.roll(centre, reach, 1), 0.0)
                near = near + jnp.where(
                    lane < AY - reach, pltpu.roll(centre, AY - reach, 1), 0.0
                )
                total = total + STENCIL[reach] * near
            if f == 0:
                here = source_ref[0] - (z + half * SLAB) * (AX * AY)
                total = total + jnp.where(flat == here, wavelet_ref[0, k], 0.0)
            else:
                total = total + injected[k, z]
            state[f, k + 2, slot, inner, :] = (
                2.0 * centre - state[f, k, slot, inner, :] + coefficient[z] * total
            )
            return carry

        lax.fori_loop(0, REACH, layer, 0)

    far, edge = REACH * half, REACH - REACH * half
    for k in range(STEPS):
        layers(0, k, far)
        layers(1, k, far)
        for f in range(2):
            halos[f, k + 1].wait_recv()
            layers(f, k, edge)
            if k + 1 < STEPS:
                halos[f, k + 2] = halo_copy(f, k + 2)
                halos[f, k + 2].start()

    def correlate(z, carry):
        slot = z + REACH
        image = state[0, 2, slot, inner, :] * state[1, STEPS + 1, slot, inner, :]
        for t in range(1, STEPS):
            image = image + state[0, t + 2, slot, inner, :] * state[1, STEPS + 1 - t, slot, inner, :]
        placed[z, pl.ds(AX, AX), :] = pltpu.roll(image * (1.0 / STEPS), b, 1)
        return carry

    lax.fori_loop(0, SLAB, correlate, 0)

    image_copies = []
    for away in range(1, SHOTS):
        owner = (me + away) % SHOTS
        outgoing[away] = placed[:, pl.ds(AX - a + owner * ROWS, ROWS), :]
        copy = pltpu.make_async_remote_copy(
            src_ref=outgoing.at[away],
            dst_ref=incoming.at[away],
            send_sem=image_send.at[away],
            recv_sem=image_recv.at[away],
            device_id={"shot": owner},
            device_id_type=MESH,
        )
        copy.start()
        image_copies.append(copy)
    strip = placed[:, pl.ds(AX - a + me * ROWS, ROWS), :]
    kept = jnp.where(lane >= b, strip, 0.0)
    left, right = kept, strip - kept
    for away in range(1, SHOTS):
        offset_copies[away - 1].wait_recv()
        image_copies[away - 1].wait_recv()
        sender = (me + SHOTS - away) % SHOTS
        strip = incoming[away]
        kept = jnp.where(lane >= offsets[sender, 0:1, :], strip, 0.0)
        left, right = left + kept, right + (strip - kept)
    out_ref[:, :, 0:AY] = left
    out_ref[:, :, AY:GY] = right[:, :, 0:TAIL]

    for copy in model_copies + offset_copies + image_copies + list(halos.values()):
        copy.wait_send()


def fused_shards(
    forward_field,
    forward_older,
    adjoint_field,
    adjoint_newer,
    velocity,
    anchor_first,
    anchor_second,
    wavelet,
    source_cell,
    receivers,
    traces,
):
    scalars = pl.BlockSpec(memory_space=pltpu.SMEM)
    vectors = pl.BlockSpec(memory_space=pltpu.VMEM)
    return pl.pallas_call(
        window_kernel,
        out_shape=jax.ShapeDtypeStruct((SLAB, ROWS, GY), jnp.float32),
        in_specs=[scalars] * 4 + [vectors] * 7,
        out_specs=vectors,
        scratch_shapes=[
            pltpu.VMEM((2, STEPS + 2, SLAB + 2 * REACH, AX + 2 * PAD, AY), jnp.float32),
            pltpu.VMEM((SLAB + SLAB // 2, GX, AY), jnp.float32),
            pltpu.VMEM((SLAB, AX, AY), jnp.float32),
            pltpu.VMEM((STEPS, SLAB, AX, AY), jnp.float32),
            pltpu.VMEM((SLAB, AX + GX, AY), jnp.float32),
            pltpu.VMEM((SHOTS, SLAB, ROWS, AY), jnp.float32),
            pltpu.VMEM((SHOTS, SLAB, ROWS, AY), jnp.float32),
            pltpu.VMEM((SHOTS, 8, AY), jnp.int32),
            pltpu.VMEM((8, AY), jnp.int32),
            pltpu.SemaphoreType.DMA((2, STEPS)),
            pltpu.SemaphoreType.DMA((2, STEPS)),
            pltpu.SemaphoreType.DMA((2 * LEVELS - 1,)),
            pltpu.SemaphoreType.DMA((SHOTS,)),
            pltpu.SemaphoreType.DMA((SHOTS,)),
            pltpu.SemaphoreType.DMA((SHOTS,)),
            pltpu.SemaphoreType.DMA((SHOTS,)),
            pltpu.SemaphoreType.DMA((SHOTS,)),
        ],
        compiler_params=pltpu.CompilerParams(
            collective_id=0, has_side_effects=True, vmem_limit_bytes=40 << 20
        ),
    )(
        anchor_first,
        anchor_second,
        wavelet,
        source_cell,
        receivers,
        traces,
        forward_field,
        forward_older,
        adjoint_field,
        adjoint_newer,
        velocity,
    )


def fits_kernel(mesh):
    return mesh.shape["shot"] == SHOTS and mesh.shape["ap"] == 2


def solution(mesh):
    body = fused_shards if fits_kernel(mesh) else shards
    in_specs = (
        P(("groups", "shot"), "ap", None, None),
        P(("groups", "shot"), "ap", None, None),
        P(("groups", "shot"), "ap", None, None),
        P(("groups", "shot"), "ap", None, None),
        P(("groups", "ap"), "shot", None),
        P(("groups", "shot")),
        P(("groups", "shot")),
        P(("groups", "shot"), None),
        P(("groups", "shot")),
        P(("groups", "shot"), None),
        P(("groups", "shot"), None, None),
    )
    out_specs = P(("groups", "ap"), "shot", None)
    return jax.shard_map(body, mesh=mesh, in_specs=in_specs, out_specs=out_specs, check_vma=False)
```

```python
import jax
import jax.numpy as jnp
from jax import lax
from jax.experimental import pallas as pl
from jax.experimental.pallas import tpu as pltpu
from jax.sharding import PartitionSpec as P

STEPS = 4
GX = 128
GY = 192


STENCIL = (-205.0 / 72.0, 8.0 / 5.0, -1.0 / 5.0, 8.0 / 315.0, -1.0 / 560.0)


def with_halo(shard, sides, width):
    for axis, dim in sides:
        count, length = (lax.axis_size(axis), shard.shape[dim])
        up = [(i, (i + 1) % count) for i in range(count - 1)]
        down = [(j, i) for i, j in up]
        last = lax.slice_in_dim(shard, length - width, length, axis=dim)
        initial = lax.slice_in_dim(shard, 0, width, axis=dim)
        before = lax.ppermute(last, axis, up)
        after = lax.ppermute(initial, axis, down)
        shard = jnp.concatenate([before, shard, after], axis=dim)
    return shard


def laplace_rows(extended):
    row_count = extended.shape[1] - 8
    width_x = extended.shape[2]
    width_y = extended.shape[3]
    padded = jnp.pad(extended, ((0, 0), (0, 0), (4, 4), (4, 4)))

    def shifted(dz, dx, dy):
        return padded[
            :, 4 + dz : 4 + dz + row_count, 4 + dx : 4 + dx + width_x, 4 + dy : 4 + dy + width_y
        ]

    summed = 3.0 * STENCIL[0] * shifted(0, 0, 0)
    for reach in range(1, 5):
        summed = summed + STENCIL[reach] * (
            shifted(reach, 0, 0)
            + shifted(-reach, 0, 0)
            + shifted(0, reach, 0)
            + shifted(0, -reach, 0)
            + shifted(0, 0, reach)
            + shifted(0, 0, -reach)
        )
    return summed


def inject(cells, amounts, start_row, row_count, width_x, width_y):
    plane = width_x * width_y
    offset_cells = cells - start_row * plane
    inside = (offset_cells >= 0) & (offset_cells < row_count * plane)
    flat = (
        jnp.zeros((row_count * plane,), jnp.float32)
        .at[jnp.where(inside, offset_cells, 0)]
        .add(jnp.where(inside, amounts, 0.0))
    )
    return flat.reshape(row_count, width_x, width_y)


def sources_for(injections, start_row, row_count, width_x, width_y):
    return jnp.stack(
        [
            inject(cells, amounts, start_row, row_count, width_x, width_y)
            for cells, amounts in injections
        ]
    )


def advance(current, previous, coefficient, injections, first_row):
    slab_rows, width_x, width_y = (current.shape[1], current.shape[2], current.shape[3])
    extended = with_halo(current, (("ap", 1),), 4)
    sources = sources_for(injections, first_row, slab_rows, width_x, width_y)
    return 2.0 * current - previous + coefficient[None] * (laplace_rows(extended) + sources)


def march(current, previous, coefficient, injections_at, first_row):
    snapshots = []
    for t in range(STEPS):
        updated = advance(current, previous, coefficient, injections_at(t), first_row)
        previous, current = (current, updated)
        snapshots.append(current)
    return snapshots


def shards(
    forward_field,
    forward_older,
    adjoint_field,
    adjoint_newer,
    velocity,
    anchor_first,
    anchor_second,
    wavelet,
    source_cell,
    receivers,
    traces,
):
    slab_rows, width_x, width_y = (
        forward_field.shape[1],
        forward_field.shape[2],
        forward_field.shape[3],
    )
    first_row = lax.axis_index("ap") * slab_rows
    anchor = anchor_first[0] * 0
    speed_model = lax.all_gather(velocity, "shot", axis=1, tiled=True)
    window = lax.dynamic_slice(
        speed_model, (anchor, anchor_first[0], anchor_second[0]), (slab_rows, width_x, width_y)
    )
    coefficient = window * window
    f_now, f_old, a_now, a_new = (forward_field, forward_older, adjoint_field, adjoint_newer)

    def forward_source(t):
        return (source_cell, wavelet[0, t : t + 1])

    def adjoint_source(t):
        return (receivers[0], traces[0, STEPS - 1 - t])

    forward_snaps = march(
        f_now.astype(jnp.float32),
        f_old.astype(jnp.float32),
        coefficient,
        lambda t: [forward_source(t)],
        first_row,
    )
    adjoint_snaps = march(
        a_now.astype(jnp.float32),
        a_new.astype(jnp.float32),
        coefficient,
        lambda t: [adjoint_source(t)],
        first_row,
    )
    forward_states = [state[0] for state in forward_snaps]
    adjoint_states = [state[0] for state in adjoint_snaps]
    correlation = forward_states[0] * adjoint_states[STEPS - 1]
    for t in range(1, STEPS):
        correlation = correlation + forward_states[t] * adjoint_states[STEPS - 1 - t]
    shot_image = correlation / STEPS
    partial_image = lax.dynamic_update_slice(
        jnp.zeros((slab_rows, GX, GY), jnp.float32),
        shot_image,
        (anchor, anchor_first[0], anchor_second[0]),
    )
    return lax.psum_scatter(partial_image, "shot", scatter_dimension=1, tiled=True)


SLAB, AX, AY = 8, 64, 128
COLUMNS, LEVELS = 2, 4
SHOTS = COLUMNS * LEVELS
ROWS = GX // SHOTS
TAIL = GY - AY
PAD = 8
REACH = 4
UNROLL = 4
MESH = pl.DeviceIdType.MESH


def window_kernel(
    a_hbm,
    b_hbm,
    wavelet_hbm,
    source_hbm,
    receivers_hbm,
    traces_hbm,
    forward_hbm,
    forward_older_hbm,
    adjoint_hbm,
    adjoint_newer_hbm,
    velocity_hbm,
    out_ref,
    a_ref,
    b_ref,
    wavelet_ref,
    source_ref,
    receivers_ref,
    traces_ref,
    forward_ref,
    forward_older_ref,
    adjoint_ref,
    adjoint_newer_ref,
    velocity_ref,
    load_sem,
    state,
    model,
    coefficient,
    injected,
    placed,
    outgoing,
    incoming,
    offsets,
    offset_tile,
    halo_send,
    halo_recv,
    model_send,
    model_recv,
    image_send,
    image_recv,
    offset_send,
    offset_recv,
):
    half = lax.axis_index("ap")
    me = lax.axis_index("shot")
    level, column = me // COLUMNS, me % COLUMNS

    barrier = pltpu.get_barrier_semaphore()
    pl.semaphore_signal(barrier, inc=1, device_id={"ap": 1 - half}, device_id_type=MESH)
    for away in range(1, SHOTS):
        pl.semaphore_signal(
            barrier, inc=1, device_id={"shot": (me + away) % SHOTS}, device_id_type=MESH
        )

    loads = []
    for source, target in (
        (velocity_hbm, velocity_ref),
        (b_hbm, b_ref),
        (forward_hbm, forward_ref),
        (adjoint_hbm, adjoint_ref),
        (receivers_hbm, receivers_ref),
        (traces_hbm, traces_ref),
        (forward_older_hbm, forward_older_ref),
        (adjoint_newer_hbm, adjoint_newer_ref),
        (a_hbm, a_ref),
        (wavelet_hbm, wavelet_ref),
        (source_hbm, source_ref),
    ):
        load = pltpu.make_async_copy(source, target, load_sem.at[len(loads)])
        load.start()
        loads.append(load)

    lane = lax.broadcasted_iota(jnp.int32, (1, AY), 1)

    outer = pl.ds((REACH + SLAB) * half, REACH)
    inner = pl.ds(PAD, AX)
    for f in range(2):
        for k in range(1, STEPS + 1):

            def clear(z, carry):
                state[f, k, z + REACH, 0:PAD, :] = jnp.zeros((PAD, AY), jnp.float32)
                state[f, k, z + REACH, PAD + AX :, :] = jnp.zeros((PAD, AY), jnp.float32)
                return carry

            lax.fori_loop(0, SLAB, clear, 0)
            state[f, k, outer, inner, :] = jnp.zeros((REACH, AX, AY), jnp.float32)

    def blank(z, carry):
        placed[z, 0:AX, :] = jnp.zeros((AX, AY), jnp.float32)
        placed[z, 2 * AX :, :] = jnp.zeros((GX - AX, AY), jnp.float32)
        return carry

    loads[0].wait()

    mine = pl.ds(pl.multiple_of(me * ROWS, ROWS), ROWS)
    for z in range(SLAB):
        model[z, mine, :] = velocity_ref[z, :, 0:AY]
    for z in range(SLAB // 2):
        model[SLAB + z, mine, :] = jnp.concatenate(
            [velocity_ref[z, :, AY:GY], velocity_ref[z + SLAB // 2, :, AY:GY]], axis=1
        )
    loads[1].wait()
    b = b_ref[0]
    offset_tile[...] = jnp.full((8, AY), b, jnp.int32)

    pl.semaphore_wait(barrier, SHOTS)

    def model_copy(block, slot, target):
        rows = pl.ds(pl.multiple_of(block * ROWS, ROWS), ROWS)
        return pltpu.make_async_remote_copy(
            src_ref=model.at[:, rows, :],
            dst_ref=model.at[:, rows, :],
            send_sem=model_send.at[slot],
            recv_sem=model_recv.at[block],
            device_id={"shot": target},
            device_id_type=MESH,
        )

    across = level * COLUMNS + 1 - column
    sends = []

    def send(block, slot, target, needed):
        copy = model_copy(block, slot, target)
        pl.when(needed)(copy.start)
        sends.append((copy, needed))

    for slot, side in enumerate((1, -1)):
        beside = level + side
        inside = jnp.logical_and(beside >= 0, beside < LEVELS)
        send(me, slot, jnp.clip(beside, 0, LEVELS - 1) * COLUMNS + column, inside)
    send(me, 2, across, level >= 0)

    def pass_on(distance):
        for side in range(2):
            step = 1 - 2 * side
            origin = level - step * distance
            there = jnp.logical_and(origin >= 0, origin < LEVELS)
            beside = level + step
            onward = jnp.logical_and(there, jnp.logical_and(beside >= 0, beside < LEVELS))
            block = jnp.clip(origin, 0, LEVELS - 1) * COLUMNS + column
            pl.when(there)(model_copy(block, 0, across).wait_recv)
            slot = 3 + 4 * (distance - 1) + 2 * side
            if distance + 1 < LEVELS:
                send(block, slot, jnp.clip(beside, 0, LEVELS - 1) * COLUMNS + column, onward)
            send(block, slot + 1, across, there)

    offset_copies = []
    for away in range(1, SHOTS):
        copy = pltpu.make_async_remote_copy(
            src_ref=offset_tile,
            dst_ref=offsets.at[me],
            send_sem=offset_send.at[away],
            recv_sem=offset_recv.at[away],
            device_id={"shot": (me + away) % SHOTS},
            device_id_type=MESH,
        )
        copy.start()
        offset_copies.append(copy)
    offsets[me] = offset_tile[...]

    def halo_copy(f, k):
        return pltpu.make_async_remote_copy(
            src_ref=state.at[f, k, pl.ds(2 * REACH - REACH * half, REACH), inner, :],
            dst_ref=state.at[f, k, pl.ds((REACH + SLAB) * half, REACH), inner, :],
            send_sem=halo_send.at[f, k - 1],
            recv_sem=halo_recv.at[f, k - 1],
            device_id={"ap": 1 - half},
            device_id_type=MESH,
        )

    halos = {}
    for f, now in enumerate((forward_ref, adjoint_ref)):
        loads[2 + f].wait()

        def widen(z, carry):
            state[f, 1, z + REACH, inner, :] = now[0, z].astype(jnp.float32)
            return carry

        lax.fori_loop(0, SLAB, widen, 0)
        halos[f, 1] = halo_copy(f, 1)
        halos[f, 1].start()
    lax.fori_loop(0, SLAB, blank, 0)
    for f, older in enumerate((forward_older_ref, adjoint_newer_ref)):
        loads[6 + f].wait()

        def widen(z, carry):
            state[f, 0, z + REACH, inner, :] = older[0, z].astype(jnp.float32)
            return carry

        lax.fori_loop(0, SLAB, widen, 0)

    loads[4].wait()
    loads[5].wait()
    cells = receivers_ref[...]
    count = cells.shape[1]
    row_of = cells // AY - half * (SLAB * AX)
    lane_of = cells % AY
    hot_rows = jnp.where(
        lax.broadcasted_iota(jnp.int32, (SLAB * AX, count), 0) == row_of, 1.0, 0.0
    ).astype(jnp.bfloat16)
    hot_lanes = lax.broadcasted_iota(jnp.int32, (AY, count), 0) == lane_of
    for k in range(STEPS):
        amounts = jnp.where(hot_lanes, traces_ref[0, STEPS - 1 - k : STEPS - k, :], 0.0)
        upper = amounts.astype(jnp.bfloat16)
        lower = (amounts - upper.astype(jnp.float32)).astype(jnp.bfloat16)
        both = lax.dot_general(
            hot_rows,
            jnp.concatenate([upper, lower], axis=0),
            (((1,), (1,)), ((), ())),
            preferred_element_type=jnp.float32,
        )
        injected[k] = (both[:, :AY] + both[:, AY:]).reshape(SLAB, AX, AY)

    for load in loads[8:]:
        load.wait()
    a = a_ref[0]
    flat = (
        lax.broadcasted_iota(jnp.int32, (AX, AY), 0) * AY
        + lax.broadcasted_iota(jnp.int32, (AX, AY), 1)
    )

    def layers(f, k, first):
        def layer(i, carry):
            z = first + i
            slot = z + REACH
            centre = state[f, k + 1, slot, inner, :]
            total = (3.0 * STENCIL[0]) * centre
            for reach in range(1, REACH + 1):
                near = state[f, k + 1, slot + reach, inner, :]
                near = near + state[f, k + 1, slot - reach, inner, :]
                near = near + state[f, k + 1, slot, pl.ds(PAD + reach, AX), :]
                near = near + state[f, k + 1, slot, pl.ds(PAD - reach, AX), :]
                near = near + jnp.where(lane >= reach, pltpu.roll(centre, reach, 1), 0.0)
                near = near + jnp.where(
                    lane < AY - reach, pltpu.roll(centre, AY - reach, 1), 0.0
                )
                total = total + STENCIL[reach] * near
            if f == 0:
                here = source_ref[0] - (z + half * SLAB) * (AX * AY)
                total = total + jnp.where(flat == here, wavelet_ref[0, k], 0.0)
            else:
                total = total + injected[k, z]
            if k > 0:
                total = 2.0 * centre - state[f, k, slot, inner, :] + coefficient[z] * total
            state[f, k + 2, slot, inner, :] = total
            return carry

        lax.fori_loop(0, REACH if k > 0 else SLAB, layer, 0, unroll=UNROLL)

    pass_on(1)
    for f in range(2):
        halos[f, 1].wait_recv()
        layers(f, 0, 0)
        pass_on(2 + f)
    for away in range(LEVELS):
        block = (level + LEVELS - away) % LEVELS * COLUMNS + 1 - column
        model_copy(block, 0, across).wait_recv()

    def square(z, carry):
        rows = pl.ds(a, AX)
        for part in range(2):
            tail = model[SLAB + z, rows, :]
            if part:
                tail = pltpu.roll(tail, TAIL, 1)
            joined = jnp.where(lane >= b, model[z + part * (SLAB // 2), rows, :], tail)
            window = pltpu.roll(joined, (AY - b) % AY, 1)
            coefficient[z + part * (SLAB // 2)] = window * window
        return carry

    lax.fori_loop(0, SLAB // 2, square, 0)

    def first_step(f, first):
        def layer(i, carry):
            slot = first + i + REACH
            state[f, 2, slot, inner, :] = (
                2.0 * state[f, 1, slot, inner, :]
                - state[f, 0, slot, inner, :]
                + coefficient[first + i] * state[f, 2, slot, inner, :]
            )
            return carry

        lax.fori_loop(0, REACH, layer, 0)

    far, edge = REACH * half, REACH - REACH * half
    for f in range(2):
        first_step(f, edge)
        halos[f, 2] = halo_copy(f, 2)
        halos[f, 2].start()
    for f in range(2):
        first_step(f, far)
    for k in range(1, STEPS):
        layers(0, k, far)
        layers(1, k, far)
        for f in range(2):
            halos[f, k + 1].wait_recv()
            layers(f, k, edge)
            if k + 1 < STEPS:
                halos[f, k + 2] = halo_copy(f, k + 2)
                halos[f, k + 2].start()

    def correlate(z, carry):
        slot = z + REACH
        image = state[0, 2, slot, inner, :] * state[1, STEPS + 1, slot, inner, :]
        for t in range(1, STEPS):
            image = image + state[0, t + 2, slot, inner, :] * state[1, STEPS + 1 - t, slot, inner, :]
        placed[z, pl.ds(AX, AX), :] = pltpu.roll(image * (1.0 / STEPS), b, 1)
        return carry

    lax.fori_loop(0, SLAB, correlate, 0)

    image_copies = []
    for away in range(1, SHOTS):
        owner = (me + away) % SHOTS
        outgoing[away] = placed[:, pl.ds(AX - a + owner * ROWS, ROWS), :]
        copy = pltpu.make_async_remote_copy(
            src_ref=outgoing.at[away],
            dst_ref=incoming.at[away],
            send_sem=image_send.at[away],
            recv_sem=image_recv.at[away],
            device_id={"shot": owner},
            device_id_type=MESH,
        )
        copy.start()
        image_copies.append(copy)
    strip = placed[:, pl.ds(AX - a + me * ROWS, ROWS), :]
    kept = jnp.where(lane >= b, strip, 0.0)
    left, right = kept, strip - kept
    for away in range(1, SHOTS):
        offset_copies[away - 1].wait_recv()
        image_copies[away - 1].wait_recv()
        sender = (me + SHOTS - away) % SHOTS
        strip = incoming[away]
        kept = jnp.where(lane >= offsets[sender, 0:1, :], strip, 0.0)
        left, right = left + kept, right + (strip - kept)
    out_ref[:, :, 0:AY] = left
    out_ref[:, :, AY:GY] = right[:, :, 0:TAIL]

    for copy, needed in sends:
        pl.when(needed)(copy.wait_send)
    for copy in offset_copies + image_copies + list(halos.values()):
        copy.wait_send()


def fused_shards(
    forward_field,
    forward_older,
    adjoint_field,
    adjoint_newer,
    velocity,
    anchor_first,
    anchor_second,
    wavelet,
    source_cell,
    receivers,
    traces,
):
    return pl.pallas_call(
        window_kernel,
        out_shape=jax.ShapeDtypeStruct((SLAB, ROWS, GY), jnp.float32),
        in_specs=[pl.BlockSpec(memory_space=pl.ANY)] * 11,
        out_specs=pl.BlockSpec(memory_space=pltpu.VMEM),
        scratch_shapes=[
            pltpu.SMEM((1,), jnp.int32),
            pltpu.SMEM((1,), jnp.int32),
            pltpu.SMEM(wavelet.shape, jnp.float32),
            pltpu.SMEM((1,), jnp.int32),
            pltpu.VMEM(receivers.shape, jnp.int32),
            pltpu.VMEM(traces.shape, jnp.float32),
            pltpu.VMEM(forward_field.shape, jnp.bfloat16),
            pltpu.VMEM(forward_field.shape, jnp.bfloat16),
            pltpu.VMEM(forward_field.shape, jnp.bfloat16),
            pltpu.VMEM(forward_field.shape, jnp.bfloat16),
            pltpu.VMEM(velocity.shape, jnp.float32),
            pltpu.SemaphoreType.DMA((11,)),
            pltpu.VMEM((2, STEPS + 2, SLAB + 2 * REACH, AX + 2 * PAD, AY), jnp.float32),
            pltpu.VMEM((SLAB + SLAB // 2, GX, AY), jnp.float32),
            pltpu.VMEM((SLAB, AX, AY), jnp.float32),
            pltpu.VMEM((STEPS, SLAB, AX, AY), jnp.float32),
            pltpu.VMEM((SLAB, AX + GX, AY), jnp.float32),
            pltpu.VMEM((SHOTS, SLAB, ROWS, AY), jnp.float32),
            pltpu.VMEM((SHOTS, SLAB, ROWS, AY), jnp.float32),
            pltpu.VMEM((SHOTS, 8, AY), jnp.int32),
            pltpu.VMEM((8, AY), jnp.int32),
            pltpu.SemaphoreType.DMA((2, STEPS)),
            pltpu.SemaphoreType.DMA((2, STEPS)),
            pltpu.SemaphoreType.DMA((3 + 4 * (LEVELS - 1),)),
            pltpu.SemaphoreType.DMA((SHOTS,)),
            pltpu.SemaphoreType.DMA((SHOTS,)),
            pltpu.SemaphoreType.DMA((SHOTS,)),
            pltpu.SemaphoreType.DMA((SHOTS,)),
            pltpu.SemaphoreType.DMA((SHOTS,)),
        ],
        compiler_params=pltpu.CompilerParams(
            collective_id=0, has_side_effects=True, vmem_limit_bytes=63 << 20
        ),
    )(
        anchor_first,
        anchor_second,
        wavelet,
        source_cell,
        receivers,
        traces,
        forward_field,
        forward_older,
        adjoint_field,
        adjoint_newer,
        velocity,
    )


def fits_kernel(mesh):
    return mesh.shape["shot"] == SHOTS and mesh.shape["ap"] == 2


def solution(mesh):
    body = fused_shards if fits_kernel(mesh) else shards
    in_specs = (
        P(("groups", "shot"), "ap", None, None),
        P(("groups", "shot"), "ap", None, None),
        P(("groups", "shot"), "ap", None, None),
        P(("groups", "shot"), "ap", None, None),
        P(("groups", "ap"), "shot", None),
        P(("groups", "shot")),
        P(("groups", "shot")),
        P(("groups", "shot"), None),
        P(("groups", "shot")),
        P(("groups", "shot"), None),
        P(("groups", "shot"), None, None),
    )
    out_specs = P(("groups", "ap"), "shot", None)
    return jax.shard_map(body, mesh=mesh, in_specs=in_specs, out_specs=out_specs, check_vma=False)
```

```python
import jax
import jax.numpy as jnp
from jax import lax
from jax.experimental import pallas as pl
from jax.experimental.pallas import tpu as pltpu
from jax.sharding import PartitionSpec as P

STEPS = 4
GX = 128
GY = 192


STENCIL = (-205.0 / 72.0, 8.0 / 5.0, -1.0 / 5.0, 8.0 / 315.0, -1.0 / 560.0)


def with_halo(shard, sides, width):
    for axis, dim in sides:
        count, length = (lax.axis_size(axis), shard.shape[dim])
        up = [(i, (i + 1) % count) for i in range(count - 1)]
        down = [(j, i) for i, j in up]
        last = lax.slice_in_dim(shard, length - width, length, axis=dim)
        initial = lax.slice_in_dim(shard, 0, width, axis=dim)
        before = lax.ppermute(last, axis, up)
        after = lax.ppermute(initial, axis, down)
        shard = jnp.concatenate([before, shard, after], axis=dim)
    return shard


def laplace_rows(extended):
    row_count = extended.shape[1] - 8
    width_x = extended.shape[2]
    width_y = extended.shape[3]
    padded = jnp.pad(extended, ((0, 0), (0, 0), (4, 4), (4, 4)))

    def shifted(dz, dx, dy):
        return padded[
            :, 4 + dz : 4 + dz + row_count, 4 + dx : 4 + dx + width_x, 4 + dy : 4 + dy + width_y
        ]

    summed = 3.0 * STENCIL[0] * shifted(0, 0, 0)
    for reach in range(1, 5):
        summed = summed + STENCIL[reach] * (
            shifted(reach, 0, 0)
            + shifted(-reach, 0, 0)
            + shifted(0, reach, 0)
            + shifted(0, -reach, 0)
            + shifted(0, 0, reach)
            + shifted(0, 0, -reach)
        )
    return summed


def inject(cells, amounts, start_row, row_count, width_x, width_y):
    plane = width_x * width_y
    offset_cells = cells - start_row * plane
    inside = (offset_cells >= 0) & (offset_cells < row_count * plane)
    flat = (
        jnp.zeros((row_count * plane,), jnp.float32)
        .at[jnp.where(inside, offset_cells, 0)]
        .add(jnp.where(inside, amounts, 0.0))
    )
    return flat.reshape(row_count, width_x, width_y)


def sources_for(injections, start_row, row_count, width_x, width_y):
    return jnp.stack(
        [
            inject(cells, amounts, start_row, row_count, width_x, width_y)
            for cells, amounts in injections
        ]
    )


def advance(current, previous, coefficient, injections, first_row):
    slab_rows, width_x, width_y = (current.shape[1], current.shape[2], current.shape[3])
    extended = with_halo(current, (("ap", 1),), 4)
    sources = sources_for(injections, first_row, slab_rows, width_x, width_y)
    return 2.0 * current - previous + coefficient[None] * (laplace_rows(extended) + sources)


def march(current, previous, coefficient, injections_at, first_row):
    snapshots = []
    for t in range(STEPS):
        updated = advance(current, previous, coefficient, injections_at(t), first_row)
        previous, current = (current, updated)
        snapshots.append(current)
    return snapshots


def shards(
    forward_field,
    forward_older,
    adjoint_field,
    adjoint_newer,
    velocity,
    anchor_first,
    anchor_second,
    wavelet,
    source_cell,
    receivers,
    traces,
):
    slab_rows, width_x, width_y = (
        forward_field.shape[1],
        forward_field.shape[2],
        forward_field.shape[3],
    )
    first_row = lax.axis_index("ap") * slab_rows
    anchor = anchor_first[0] * 0
    speed_model = lax.all_gather(velocity, "shot", axis=1, tiled=True)
    window = lax.dynamic_slice(
        speed_model, (anchor, anchor_first[0], anchor_second[0]), (slab_rows, width_x, width_y)
    )
    coefficient = window * window
    f_now, f_old, a_now, a_new = (forward_field, forward_older, adjoint_field, adjoint_newer)

    def forward_source(t):
        return (source_cell, wavelet[0, t : t + 1])

    def adjoint_source(t):
        return (receivers[0], traces[0, STEPS - 1 - t])

    forward_snaps = march(
        f_now.astype(jnp.float32),
        f_old.astype(jnp.float32),
        coefficient,
        lambda t: [forward_source(t)],
        first_row,
    )
    adjoint_snaps = march(
        a_now.astype(jnp.float32),
        a_new.astype(jnp.float32),
        coefficient,
        lambda t: [adjoint_source(t)],
        first_row,
    )
    forward_states = [state[0] for state in forward_snaps]
    adjoint_states = [state[0] for state in adjoint_snaps]
    correlation = forward_states[0] * adjoint_states[STEPS - 1]
    for t in range(1, STEPS):
        correlation = correlation + forward_states[t] * adjoint_states[STEPS - 1 - t]
    shot_image = correlation / STEPS
    partial_image = lax.dynamic_update_slice(
        jnp.zeros((slab_rows, GX, GY), jnp.float32),
        shot_image,
        (anchor, anchor_first[0], anchor_second[0]),
    )
    return lax.psum_scatter(partial_image, "shot", scatter_dimension=1, tiled=True)


SLAB, AX, AY = 8, 64, 128
COLUMNS, LEVELS = 2, 4
SHOTS = COLUMNS * LEVELS
ROWS = GX // SHOTS
TAIL = GY - AY
PAD = 8
REACH = 4
UNROLL = 4
MESH = pl.DeviceIdType.MESH


def window_kernel(
    a_hbm,
    b_hbm,
    wavelet_hbm,
    source_hbm,
    receivers_hbm,
    traces_hbm,
    forward_hbm,
    forward_older_hbm,
    adjoint_hbm,
    adjoint_newer_hbm,
    velocity_hbm,
    out_ref,
    a_ref,
    b_ref,
    wavelet_ref,
    source_ref,
    receivers_ref,
    traces_ref,
    forward_ref,
    forward_older_ref,
    adjoint_ref,
    adjoint_newer_ref,
    velocity_ref,
    load_sem,
    state,
    model,
    coefficient,
    injected,
    placed,
    outgoing,
    incoming,
    offsets,
    offset_tile,
    halo_send,
    halo_recv,
    model_send,
    model_recv,
    image_send,
    image_recv,
    offset_send,
    offset_recv,
):
    half = lax.axis_index("ap")
    me = lax.axis_index("shot")
    level, column = me // COLUMNS, me % COLUMNS

    barrier = pltpu.get_barrier_semaphore()
    pl.semaphore_signal(barrier, inc=1, device_id={"ap": 1 - half}, device_id_type=MESH)
    for away in range(1, SHOTS):
        pl.semaphore_signal(
            barrier, inc=1, device_id={"shot": (me + away) % SHOTS}, device_id_type=MESH
        )

    loads = []
    for source, target in (
        (velocity_hbm, velocity_ref),
        (b_hbm, b_ref),
        (forward_hbm, forward_ref),
        (adjoint_hbm, adjoint_ref),
        (receivers_hbm, receivers_ref),
        (traces_hbm, traces_ref),
        (forward_older_hbm, forward_older_ref),
        (adjoint_newer_hbm, adjoint_newer_ref),
        (a_hbm, a_ref),
        (wavelet_hbm, wavelet_ref),
        (source_hbm, source_ref),
    ):
        load = pltpu.make_async_copy(source, target, load_sem.at[len(loads)])
        load.start()
        loads.append(load)

    lane = lax.broadcasted_iota(jnp.int32, (1, AY), 1)

    outer = pl.ds((REACH + SLAB) * half, REACH)
    inner = pl.ds(PAD, AX)
    for f in range(2):
        for k in range(1, STEPS + 1):

            def clear(z, carry):
                state[f, k, z + REACH, 0:PAD, :] = jnp.zeros((PAD, AY), jnp.float32)
                state[f, k, z + REACH, PAD + AX :, :] = jnp.zeros((PAD, AY), jnp.float32)
                return carry

            lax.fori_loop(0, SLAB, clear, 0)
            state[f, k, outer, inner, :] = jnp.zeros((REACH, AX, AY), jnp.float32)

    def blank(z, carry):
        placed[z, 0:AX, :] = jnp.zeros((AX, AY), jnp.float32)
        placed[z, 2 * AX :, :] = jnp.zeros((GX - AX, AY), jnp.float32)
        return carry

    loads[0].wait()

    mine = pl.ds(pl.multiple_of(me * ROWS, ROWS), ROWS)
    for z in range(SLAB):
        model[z, mine, :] = velocity_ref[z, :, 0:AY]
    for z in range(SLAB // 2):
        model[SLAB + z, mine, :] = jnp.concatenate(
            [velocity_ref[z, :, AY:GY], velocity_ref[z + SLAB // 2, :, AY:GY]], axis=1
        )
    loads[1].wait()
    b = b_ref[0]
    offset_tile[...] = jnp.full((8, AY), b, jnp.int32)

    pl.semaphore_wait(barrier, SHOTS)

    def model_copy(block, slot, target):
        rows = pl.ds(pl.multiple_of(block * ROWS, ROWS), ROWS)
        return pltpu.make_async_remote_copy(
            src_ref=model.at[:, rows, :],
            dst_ref=model.at[:, rows, :],
            send_sem=model_send.at[slot],
            recv_sem=model_recv.at[block],
            device_id={"shot": target},
            device_id_type=MESH,
        )

    across = level * COLUMNS + 1 - column
    sends = []

    def send(block, slot, target, needed):
        copy = model_copy(block, slot, target)
        pl.when(needed)(copy.start)
        sends.append((copy, needed))

    for slot, side in enumerate((1, -1)):
        beside = level + side
        inside = jnp.logical_and(beside >= 0, beside < LEVELS)
        send(me, slot, jnp.clip(beside, 0, LEVELS - 1) * COLUMNS + column, inside)
    send(me, 2, across, level >= 0)

    def pass_on(distance):
        for side in range(2):
            step = 1 - 2 * side
            origin = level - step * distance
            there = jnp.logical_and(origin >= 0, origin < LEVELS)
            beside = level + step
            onward = jnp.logical_and(there, jnp.logical_and(beside >= 0, beside < LEVELS))
            block = jnp.clip(origin, 0, LEVELS - 1) * COLUMNS + column
            pl.when(there)(model_copy(block, 0, across).wait_recv)
            slot = 3 + 4 * (distance - 1) + 2 * side
            if distance + 1 < LEVELS:
                send(block, slot, jnp.clip(beside, 0, LEVELS - 1) * COLUMNS + column, onward)
            send(block, slot + 1, across, there)

    offset_copies = []
    for away in range(1, SHOTS):
        copy = pltpu.make_async_remote_copy(
            src_ref=offset_tile,
            dst_ref=offsets.at[me],
            send_sem=offset_send.at[away],
            recv_sem=offset_recv.at[away],
            device_id={"shot": (me + away) % SHOTS},
            device_id_type=MESH,
        )
        copy.start()
        offset_copies.append(copy)
    offsets[me] = offset_tile[...]

    def halo_copy(f, k):
        return pltpu.make_async_remote_copy(
            src_ref=state.at[f, k, pl.ds(2 * REACH - REACH * half, REACH), inner, :],
            dst_ref=state.at[f, k, pl.ds((REACH + SLAB) * half, REACH), inner, :],
            send_sem=halo_send.at[f, k - 1],
            recv_sem=halo_recv.at[f, k - 1],
            device_id={"ap": 1 - half},
            device_id_type=MESH,
        )

    halos = {}
    for f, now in enumerate((forward_ref, adjoint_ref)):
        loads[2 + f].wait()

        def widen(z, carry):
            state[f, 1, z + REACH, inner, :] = now[0, z].astype(jnp.float32)
            return carry

        lax.fori_loop(0, SLAB, widen, 0)
        halos[f, 1] = halo_copy(f, 1)
        halos[f, 1].start()
    lax.fori_loop(0, SLAB, blank, 0)
    for f, older in enumerate((forward_older_ref, adjoint_newer_ref)):
        loads[6 + f].wait()

        def widen(z, carry):
            state[f, 0, z + REACH, inner, :] = older[0, z].astype(jnp.float32)
            return carry

        lax.fori_loop(0, SLAB, widen, 0)

    loads[4].wait()
    loads[5].wait()
    cells = receivers_ref[...]
    count = cells.shape[1]
    row_of = cells // AY - half * (SLAB * AX)
    lane_of = cells % AY
    hot_rows = jnp.where(
        lax.broadcasted_iota(jnp.int32, (SLAB * AX, count), 0) == row_of, 1.0, 0.0
    ).astype(jnp.bfloat16)
    hot_lanes = lax.broadcasted_iota(jnp.int32, (AY, count), 0) == lane_of
    for k in range(STEPS):
        amounts = jnp.where(hot_lanes, traces_ref[0, STEPS - 1 - k : STEPS - k, :], 0.0)
        upper = amounts.astype(jnp.bfloat16)
        lower = (amounts - upper.astype(jnp.float32)).astype(jnp.bfloat16)
        both = lax.dot_general(
            hot_rows,
            jnp.concatenate([upper, lower], axis=0),
            (((1,), (1,)), ((), ())),
            preferred_element_type=jnp.float32,
        )
        injected[k] = (both[:, :AY] + both[:, AY:]).reshape(SLAB, AX, AY)

    for load in loads[8:]:
        load.wait()
    a = a_ref[0]
    flat = (
        lax.broadcasted_iota(jnp.int32, (AX, AY), 0) * AY
        + lax.broadcasted_iota(jnp.int32, (AX, AY), 1)
    )

    def layers(f, k, first):
        def layer(i, carry):
            z = first + i
            slot = z + REACH
            centre = state[f, k + 1, slot, inner, :]
            total = (3.0 * STENCIL[0]) * centre
            for reach in range(1, REACH + 1):
                near = state[f, k + 1, slot + reach, inner, :]
                near = near + state[f, k + 1, slot - reach, inner, :]
                near = near + state[f, k + 1, slot, pl.ds(PAD + reach, AX), :]
                near = near + state[f, k + 1, slot, pl.ds(PAD - reach, AX), :]
                near = near + jnp.where(lane >= reach, pltpu.roll(centre, reach, 1), 0.0)
                near = near + jnp.where(
                    lane < AY - reach, pltpu.roll(centre, AY - reach, 1), 0.0
                )
                total = total + STENCIL[reach] * near
            if f == 0:
                here = source_ref[0] - (z + half * SLAB) * (AX * AY)
                total = total + jnp.where(flat == here, wavelet_ref[0, k], 0.0)
            else:
                total = total + injected[k, z]
            if k > 0:
                total = 2.0 * centre - state[f, k, slot, inner, :] + coefficient[z] * total
            state[f, k + 2, slot, inner, :] = total
            return carry

        lax.fori_loop(0, REACH if k > 0 else SLAB, layer, 0, unroll=UNROLL)

    pass_on(1)
    for f in range(2):
        halos[f, 1].wait_recv()
        layers(f, 0, 0)
        pass_on(2 + f)
    for away in range(LEVELS):
        block = (level + LEVELS - away) % LEVELS * COLUMNS + 1 - column
        model_copy(block, 0, across).wait_recv()

    def square(z, carry):
        rows = pl.ds(a, AX)
        for part in range(2):
            tail = model[SLAB + z, rows, :]
            if part:
                tail = pltpu.roll(tail, TAIL, 1)
            joined = jnp.where(lane >= b, model[z + part * (SLAB // 2), rows, :], tail)
            window = pltpu.roll(joined, (AY - b) % AY, 1)
            coefficient[z + part * (SLAB // 2)] = window * window
        return carry

    lax.fori_loop(0, SLAB // 2, square, 0)

    def first_step(f, first):
        def layer(i, carry):
            slot = first + i + REACH
            state[f, 2, slot, inner, :] = (
                2.0 * state[f, 1, slot, inner, :]
                - state[f, 0, slot, inner, :]
                + coefficient[first + i] * state[f, 2, slot, inner, :]
            )
            return carry

        lax.fori_loop(0, REACH, layer, 0)

    far, edge = REACH * half, REACH - REACH * half
    for f in range(2):
        first_step(f, edge)
        halos[f, 2] = halo_copy(f, 2)
        halos[f, 2].start()
    for f in range(2):
        first_step(f, far)
    def correlate(z, carry):
        slot = z + REACH
        image = state[0, 2, slot, inner, :] * state[1, STEPS + 1, slot, inner, :]
        for t in range(1, STEPS):
            image = image + state[0, t + 2, slot, inner, :] * state[1, STEPS + 1 - t, slot, inner, :]
        placed[z, pl.ds(AX, AX), :] = pltpu.roll(image * (1.0 / STEPS), b, 1)
        return carry

    image_copies = []

    def deliver(part, first):
        lax.fori_loop(first, first + REACH, correlate, 0)
        some = pl.ds(first, REACH)
        for away in range(1, SHOTS):
            owner = (me + away) % SHOTS
            outgoing[away, some] = placed[some, pl.ds(AX - a + owner * ROWS, ROWS), :]
            copy = pltpu.make_async_remote_copy(
                src_ref=outgoing.at[away, some],
                dst_ref=incoming.at[away, some],
                send_sem=image_send.at[part * SHOTS + away],
                recv_sem=image_recv.at[part * SHOTS + away],
                device_id={"shot": owner},
                device_id_type=MESH,
            )
            copy.start()
            image_copies.append(copy)

    for k in range(1, STEPS):
        layers(0, k, far)
        layers(1, k, far)
        if k + 1 == STEPS:
            deliver(0, far)
        for f in range(2):
            halos[f, k + 1].wait_recv()
            layers(f, k, edge)
            if k + 1 < STEPS:
                halos[f, k + 2] = halo_copy(f, k + 2)
                halos[f, k + 2].start()

    deliver(1, edge)
    strip = placed[:, pl.ds(AX - a + me * ROWS, ROWS), :]
    kept = jnp.where(lane >= b, strip, 0.0)
    left, right = kept, strip - kept
    for away in range(1, SHOTS):
        offset_copies[away - 1].wait_recv()
        image_copies[away - 1].wait_recv()
        image_copies[SHOTS + away - 2].wait_recv()
        sender = (me + SHOTS - away) % SHOTS
        strip = incoming[away]
        kept = jnp.where(lane >= offsets[sender, 0:1, :], strip, 0.0)
        left, right = left + kept, right + (strip - kept)
    out_ref[:, :, 0:AY] = left
    out_ref[:, :, AY:GY] = right[:, :, 0:TAIL]

    for copy, needed in sends:
        pl.when(needed)(copy.wait_send)
    for copy in offset_copies + image_copies + list(halos.values()):
        copy.wait_send()


def fused_shards(
    forward_field,
    forward_older,
    adjoint_field,
    adjoint_newer,
    velocity,
    anchor_first,
    anchor_second,
    wavelet,
    source_cell,
    receivers,
    traces,
):
    return pl.pallas_call(
        window_kernel,
        out_shape=jax.ShapeDtypeStruct((SLAB, ROWS, GY), jnp.float32),
        in_specs=[pl.BlockSpec(memory_space=pl.ANY)] * 11,
        out_specs=pl.BlockSpec(memory_space=pltpu.VMEM),
        scratch_shapes=[
            pltpu.SMEM((1,), jnp.int32),
            pltpu.SMEM((1,), jnp.int32),
            pltpu.SMEM(wavelet.shape, jnp.float32),
            pltpu.SMEM((1,), jnp.int32),
            pltpu.VMEM(receivers.shape, jnp.int32),
            pltpu.VMEM(traces.shape, jnp.float32),
            pltpu.VMEM(forward_field.shape, jnp.bfloat16),
            pltpu.VMEM(forward_field.shape, jnp.bfloat16),
            pltpu.VMEM(forward_field.shape, jnp.bfloat16),
            pltpu.VMEM(forward_field.shape, jnp.bfloat16),
            pltpu.VMEM(velocity.shape, jnp.float32),
            pltpu.SemaphoreType.DMA((11,)),
            pltpu.VMEM((2, STEPS + 2, SLAB + 2 * REACH, AX + 2 * PAD, AY), jnp.float32),
            pltpu.VMEM((SLAB + SLAB // 2, GX, AY), jnp.float32),
            pltpu.VMEM((SLAB, AX, AY), jnp.float32),
            pltpu.VMEM((STEPS, SLAB, AX, AY), jnp.float32),
            pltpu.VMEM((SLAB, AX + GX, AY), jnp.float32),
            pltpu.VMEM((SHOTS, SLAB, ROWS, AY), jnp.float32),
            pltpu.VMEM((SHOTS, SLAB, ROWS, AY), jnp.float32),
            pltpu.VMEM((SHOTS, 8, AY), jnp.int32),
            pltpu.VMEM((8, AY), jnp.int32),
            pltpu.SemaphoreType.DMA((2, STEPS)),
            pltpu.SemaphoreType.DMA((2, STEPS)),
            pltpu.SemaphoreType.DMA((3 + 4 * (LEVELS - 1),)),
            pltpu.SemaphoreType.DMA((SHOTS,)),
            pltpu.SemaphoreType.DMA((2 * SHOTS,)),
            pltpu.SemaphoreType.DMA((2 * SHOTS,)),
            pltpu.SemaphoreType.DMA((SHOTS,)),
            pltpu.SemaphoreType.DMA((SHOTS,)),
        ],
        compiler_params=pltpu.CompilerParams(
            collective_id=0, has_side_effects=True, vmem_limit_bytes=63 << 20
        ),
    )(
        anchor_first,
        anchor_second,
        wavelet,
        source_cell,
        receivers,
        traces,
        forward_field,
        forward_older,
        adjoint_field,
        adjoint_newer,
        velocity,
    )


def fits_kernel(mesh):
    return mesh.shape["shot"] == SHOTS and mesh.shape["ap"] == 2


def solution(mesh):
    body = fused_shards if fits_kernel(mesh) else shards
    in_specs = (
        P(("groups", "shot"), "ap", None, None),
        P(("groups", "shot"), "ap", None, None),
        P(("groups", "shot"), "ap", None, None),
        P(("groups", "shot"), "ap", None, None),
        P(("groups", "ap"), "shot", None),
        P(("groups", "shot")),
        P(("groups", "shot")),
        P(("groups", "shot"), None),
        P(("groups", "shot")),
        P(("groups", "shot"), None),
        P(("groups", "shot"), None, None),
    )
    out_specs = P(("groups", "ap"), "shot", None)
    return jax.shard_map(body, mesh=mesh, in_specs=in_specs, out_specs=out_specs, check_vma=False)
```
